128 devices in a mesh: group: 32 (over x_hi, z, y), blk: 4 (over x_lo, core).
Axes of the slice: x: 4 (x_hi: 2, x_lo: 2; x = x_hi * 2 + x_lo), y: 4, z: 4, core: 2. Of those that a mesh axis runs over, the one named last changes fastest.
Arguments:
- sources: bfloat16 [4, 1048576, 128], P(None, ('group', 'blk')), may hold values from -0.09375 to 0.09375
- positions: float32 [3, 1048576], P(None, ('group', 'blk')), may hold values from -1 to 1, as said below
- counts: int32 [128], P(('group', 'blk')), may hold values from 1024 to 8192, as said below
- offsets: int32 [2048, 4], P(('group', 'blk')), may hold values from 0 to 47, as said below
- observers: float32 [3, 512], P(None, 'blk'), may hold values from -1.35 to 1.35, as said below
Outputs:
- pressure: float32 [512, 128], P('blk', 'group')
The draws below stay inside these ranges and needn't reach their ends.
Inputs may be any that keep to these rules, and one draw needn't show every extreme that they name: `counts`: each block's count is at least 1024, and some block is full, with exactly 8192 live faces. `offsets`: offsets take the value 0 and the value 48 - 1 somewhere in every draw. `positions`: every face centre lies on the surface of the cube from -1 to 1: some coordinate is -1 or 1. `observers`: each observer has some coordinate of magnitude 1.25 or more.
All inputs are finite; a program needn't handle non-finite values.
Results may differ from the reference program's by a relative error of at most 0.014.
Values may be sent and summed in bfloat16 or wider, within the bound.
No kernel may reach another device: no remote copies, remote signals or barrier semaphores. Data moves between devices by JAX's collectives and lax.ppermute only.
A program may use at most 128 MiB of HBM per device.

```python
import jax
import jax.numpy as jnp
from jax import lax

TS = 128
O = 512
FB_CAP = 8192
FSUB = 512
KMAX = 48
BLOCKS = 128
FACES = 1048576
NFS = 16
NOSUB = 4


def draw_counts(key, part):
    key = jax.random.fold_in(key, 11)
    first, second = jax.random.split(key)
    base = jax.random.randint(first, (BLOCKS,), FB_CAP // 8, FB_CAP // 2 + 1)
    full_block = jax.random.randint(second, (), 0, BLOCKS)
    return jnp.where(jnp.arange(BLOCKS) == full_block, FB_CAP, base).astype(jnp.int32)


def draw_offsets(key, part):
    key = jax.random.fold_in(key, 23)
    first, second = jax.random.split(key)
    rows = BLOCKS * NFS
    values = jax.random.randint(first, (rows * NOSUB,), 0, KMAX)
    spots = jax.random.permutation(second, rows * NOSUB)
    places = jnp.arange(rows * NOSUB)
    values = jnp.where(places == spots[0], KMAX - 1, values)
    values = jnp.where(places == spots[1], 0, values)
    return values.reshape(rows, NOSUB).astype(jnp.int32)


def draw_positions(key, part):
    key = jax.random.fold_in(key, 41)
    keys = jax.random.split(key, 3)
    side = jax.random.randint(keys[0], (FACES,), 0, 3)
    sign = (jax.random.randint(keys[1], (FACES,), 0, 2) * 2 - 1).astype(jnp.float32)
    others = jax.random.uniform(keys[2], (3, FACES), jnp.float32, -1.0, 1.0)
    axis_ids = jnp.arange(3)[:, None]
    coords = jnp.where(axis_ids == side[None, :], sign[None, :], others)
    return coords.astype(jnp.float32)


def draw_observers(key, part):
    key = jax.random.fold_in(key, 37)
    keys = jax.random.split(key, 4)
    near, far, spread = (1.25, 1.35, 1.35)
    side = jax.random.randint(keys[0], (O,), 0, 3)
    sign = (jax.random.randint(keys[1], (O,), 0, 2) * 2 - 1).astype(jnp.float32)
    outward = jax.random.uniform(keys[2], (O,), jnp.float32, near, far)
    others = jax.random.uniform(keys[3], (3, O), jnp.float32, -spread, spread)
    axis_ids = jnp.arange(3)[:, None]
    coords = jnp.where(axis_ids == side[None, :], (sign * outward)[None, :], others)
    return coords.astype(jnp.float32)


def block_levels(stream_key, dims, cuts, smallest, high):
    def one(axis_at, parts):
        draws = jax.random.uniform(jax.random.fold_in(jax.random.fold_in(stream_key, 6), axis_at), (parts,), jnp.float32, smallest / len(cuts), high / len(cuts))
        return jnp.repeat(jnp.exp(draws), dims[axis_at] // parts).reshape((-1,) + (1,) * (len(dims) - axis_at - 1))

    gain = one(*cuts[0])
    for cut in cuts[1:]:
        gain = gain * one(*cut)
    return gain


def noise(own_key, extent, scale, reach, cuts=(), kind=jnp.bfloat16):
    loudness = block_levels(own_key, extent, cuts, -0.22, 0.18) if cuts else 1.0
    drawn = jax.random.normal(own_key, extent, jnp.float32) * scale * loudness
    return jnp.minimum(jnp.maximum(drawn, -reach), reach).astype(kind)


def setup_inputs(seed: int = 0) -> dict:
    seeds = jax.random.split(jax.random.key(seed), 6)
    sources = noise(seeds[0], (4, FACES, TS), (12.0 / FACES ** 0.5), 0.09375, ((1, 128),))
    positions = draw_positions(jax.random.fold_in(seeds[5], 71), 0)
    counts = draw_counts(jax.random.fold_in(seeds[5], 71), 0)
    offsets = draw_offsets(jax.random.fold_in(seeds[5], 71), 0)
    observers = draw_observers(jax.random.fold_in(seeds[5], 71), 0)
    return dict(sources=sources, positions=positions, counts=counts, offsets=offsets, observers=observers)


def make_channels(source_piece):
    loads = source_piece[1:4].astype(jnp.float32)
    padded = jnp.pad(loads, ((0, 0), (0, 0), (1, 1)))
    rate = (padded[:, :, 2:] - padded[:, :, :-2]).astype(jnp.bfloat16)
    return jnp.concatenate([source_piece, rate], 0)

def make_coeffs(face_pos, observer_pos, valid):
    diff = observer_pos[:, None, :] - face_pos[:, :, None]
    inv = lax.rsqrt(lax.optimization_barrier(jnp.sum(diff * diff, 0)))
    unit = diff * inv[None]
    coeffs = jnp.concatenate([inv[None], unit * (inv * inv)[None], unit * inv[None]], 0)
    return (coeffs * valid[None, :, None]).astype(jnp.bfloat16)

def delayed(signal, shifts):
    groups = shifts.shape[0]
    samples = signal.shape[1]
    blocks = signal.reshape(groups, signal.shape[0] // groups, samples)
    padded = jnp.concatenate([jnp.zeros_like(blocks), blocks], 2)

    def move(block, shift):
        return lax.dynamic_slice_in_dim(block, (samples - shift).astype(jnp.int32), samples, 1)
    return jax.vmap(move)(padded, shifts).reshape(signal.shape)

def sub_term(source_piece, face_pos, observer_pos, valid, shifts):
    sub = source_piece.shape[1]
    chans = make_channels(source_piece).reshape(7 * sub, source_piece.shape[2])
    coeffs = make_coeffs(face_pos, observer_pos, valid).reshape(7 * sub, observer_pos.shape[1])
    signal = lax.dot_general(coeffs, chans, (((0,), (0,)), ((), ())), preferred_element_type=jnp.float32)
    return delayed(signal, shifts)

def reference(sources, positions, counts, offsets, observers):
    nsub = FB_CAP // FSUB

    def one_block(block, total):
        block = jnp.asarray(block).astype(jnp.int32)
        live = counts[block]

        def one_sub(index, acc):
            index = jnp.asarray(index).astype(jnp.int32)
            first = index * FSUB
            start = (block * FB_CAP + first).astype(jnp.int32)
            piece = lax.dynamic_slice_in_dim(sources, start, FSUB, 1)
            face_pos = lax.dynamic_slice_in_dim(positions, start, FSUB, 1)
            shifts = offsets[block * nsub + index]
            valid = (first + jnp.arange(FSUB, dtype=jnp.int32) < live).astype(jnp.float32)
            return lax.cond(first < live, lambda a: a + sub_term(piece, face_pos, observers, valid, shifts), lambda a: a, acc)
        return lax.fori_loop(0, nsub, one_sub, total)
    total = lax.fori_loop(0, BLOCKS, one_block, jnp.zeros((O, TS), jnp.float32))
    return total * (1.0 / (4.0 * jnp.pi))
```

```python
import functools
import jax, jax.numpy as jnp
from jax import lax
from jax.experimental import pallas as pl
from jax.experimental.pallas import tpu as pltpu
from jax.sharding import PartitionSpec as P
FSUB=512
PADR=8
def kernel(live_ref, off_ref, obs_ref, pos_ref, src_ref, out_ref, c_ref, lt_ref, pb_ref, acc_ref, p2_ref, *, nsub, sps, mxu_r2=False):
    step = pl.program_id(0)
    T = src_ref.shape[2]; O = obs_ref.shape[1]; NT = O // 256
    @pl.when(step == 0)
    def _():
        acc_ref[...] = jnp.zeros_like(acc_ref)
    live = live_ref[0]
    def prep(u):
        s = step * sps + u
        left = live - s * FSUB
        keep = lax.broadcasted_iota(jnp.int32, (T, FSUB), 1) < left
        for c in range(4):
            lt = src_ref[c, u*FSUB:(u+1)*FSUB, :].T
            lt_ref[u, :, c*FSUB:(c+1)*FSUB] = jnp.where(keep, lt.astype(jnp.float32), 0.0).astype(jnp.bfloat16)
        for j in range(3):
            row = pos_ref[j:j+1, u*FSUB:(u+1)*FSUB]
            pb_ref[u, j] = jnp.broadcast_to(row, (128, FSUB)).T
    def coeffs(u, n):
        for h in range(2):
            o0 = n*256 + h*128
            ob = [jnp.broadcast_to(obs_ref[j:j+1, o0:o0+128], (16, 128)) for j in range(3)]
            for r in range(0, FSUB, 16):
                d = [ob[j] - pb_ref[u, j, r:r+16, :] for j in range(3)]
                r2 = d[0]*d[0] + d[1]*d[1] + d[2]*d[2]
                inv = lax.rsqrt(r2)
                i2 = inv*inv
                i3 = (i2*inv).astype(jnp.bfloat16)
                i2 = i2.astype(jnp.bfloat16)
                db = [x.astype(jnp.bfloat16) for x in d]
                ln = slice(h*128, h*128+128)
                def put(c, v):
                    c_ref[u, n, c*FSUB + r:c*FSUB + r + 16, ln] = v
                put(0, inv.astype(jnp.bfloat16))
                for j in range(3):
                    put(1+j, db[j]*i3)
                    put(4+j, db[j]*i2)
    def mm(u, n):
        s = step * sps + u
        p13 = jnp.dot(lt_ref[u], c_ref[u, n, :4*FSUB, :], preferred_element_type=jnp.float32)
        p2 = jnp.dot(lt_ref[u, :, FSUB:], c_ref[u, n, 4*FSUB:, :], preferred_element_type=jnp.float32)
        for h in range(2):
            q = n*2+h
            off = off_ref[s, q]
            sl = slice(h*128, h*128+128)
            a = p13[:, sl]; b = p2[:, sl]
            p2_ref[u, q, PADR:PADR+T, :] = b
            v = a + p2_ref[u, q, PADR+1:PADR+T+1, :] - p2_ref[u, q, PADR-1:PADR+T-1, :]
            acc_ref[q, pl.ds(off, T), :] += v
    @pl.when(step == 0)
    def _():
        p2_ref[...] = jnp.zeros_like(p2_ref)
    @pl.when(step * sps * FSUB < live)
    def _():
        prev = None
        for u in range(sps):
            prep(u)
            for n in range(NT):
                coeffs(u, n)
                if prev is not None: mm(*prev)
                prev = (u, n)
        mm(*prev)
    @pl.when(step == pl.num_programs(0) - 1)
    def _():
        pw = out_ref.shape[1]
        for q in range(2*NT):
            for w in range(pw):
                out_ref[pl.ds(q, T // pw, stride=2*NT), w, :] = acc_ref[q, pl.ds(w, T // pw, stride=pw), :]
def call(src, pos, live, off, obs, sps=1, pw=4):
    F = src.shape[1]; T = src.shape[2]; O = obs.shape[1]
    nsub = F // FSUB; NT = O//256
    return pl.pallas_call(
        functools.partial(kernel, nsub=nsub, sps=sps),
        out_shape=jax.ShapeDtypeStruct((T // pw * (O // 128), pw, 128), jnp.float32),
        grid=(nsub//sps,),
        in_specs=[pl.BlockSpec(memory_space=pltpu.SMEM), pl.BlockSpec(memory_space=pltpu.SMEM),
                  pl.BlockSpec((3, O), lambda i: (0, 0)),
                  pl.BlockSpec((3, sps*FSUB), lambda i: (0, i)),
                  pl.BlockSpec((4, sps*FSUB, T), lambda i: (0, i, 0))],
        out_specs=pl.BlockSpec((T // pw * (O // 128), pw, 128), lambda i: (0, 0, 0)),
        scratch_shapes=[pltpu.VMEM((sps, NT, 7*FSUB, 256), jnp.bfloat16),
                        pltpu.VMEM((sps, T, 4*FSUB), jnp.bfloat16),
                        pltpu.VMEM((sps, 3, FSUB, 128), jnp.float32),
                        pltpu.VMEM((2*NT, T + 64, 128), jnp.float32),
                        pltpu.VMEM((sps, 2*NT, T + 2*PADR, 128), jnp.float32)],
        compiler_params=pltpu.CompilerParams(vmem_limit_bytes=56*1024*1024, dimension_semantics=("arbitrary",)),
    )(live, off, obs, pos, src)


def body(sources, positions, counts, offsets, observers):
    everyone = lax.all_gather(observers, "blk", axis=1, tiled=True)
    ngroup = lax.axis_size("group")
    pieces = call(sources, positions, counts, offsets, everyone, sps=2, pw=sources.shape[2] // ngroup)
    arrived = lax.all_to_all(pieces, ("group", "blk"), 0, 0, tiled=True)
    return (arrived.sum(0) * (1.0 / (4.0 * jnp.pi))).T


def solution(mesh):
    return jax.shard_map(
        body,
        mesh=mesh,
        in_specs=(
            P(None, ("group", "blk"), None),
            P(None, ("group", "blk")),
            P(("group", "blk")),
            P(("group", "blk"), None),
            P(None, "blk"),
        ),
        out_specs=P("blk", "group"),
        check_vma=False,
    )
```

```python
import functools
import jax, jax.numpy as jnp
from jax import lax
from jax.experimental import pallas as pl
from jax.experimental.pallas import tpu as pltpu
from jax.sharding import PartitionSpec as P
FSUB=512
PADR=8
CH=64
U=2
AHEAD=4
def signal_kernel(live_hbm, off_hbm, *rest, nob, T, nsub, pw):
    obs_any = rest[:nob]
    pos_hbm, src_hbm, out_ref = rest[nob:nob+3]
    live_s, off_s, obs_v, pos_v, src_v, lt_ref, pb_ref, acc_ref, p2_ref, sem, ssem = rest[nob+3:]
    NT = nob // 2
    me = lax.axis_index("blk")
    NP = FSUB // (2*CH)
    small = [pltpu.make_async_copy(live_hbm, live_s, sem.at[0]),
             pltpu.make_async_copy(off_hbm, off_s, sem.at[1]),
             pltpu.make_async_copy(pos_hbm, pos_v, sem.at[2])]
    views = [pltpu.make_async_copy(obs_any[m], obs_v.at[m], sem.at[3+m]) for m in range(nob)]
    def load(s):
        return pltpu.make_async_copy(src_hbm.at[:, pl.ds(pl.multiple_of(s*FSUB, FSUB), FSUB), :], src_v.at[s], ssem.at[s])
    small[0].start()
    small[2].start()
    load(0).start()
    small[1].start()
    for c in views: c.start()
    load(1).start()
    acc_ref[...] = jnp.zeros_like(acc_ref)
    for m in range(nob):
        for u in range(U):
            p2_ref[u, m, 0:PADR, :] = jnp.zeros((PADR, 128), jnp.float32)
            p2_ref[u, m, PADR+T:, :] = jnp.zeros((PADR, 128), jnp.float32)
    small[0].wait()
    live = live_s[0]
    nlive = lax.div(live + FSUB - 1, FSUB)
    for s in range(2, AHEAD):
        @pl.when(s < nlive)
        def _(): load(s).start()
    def prep(s, kk):
        for e in range(2):
            f0 = (2*kk+e)*CH
            x = jnp.concatenate([src_v[s, c, f0:f0+CH, :] for c in (1, 2, 3, 0)], 0)
            lt_ref[2*kk+e] = x.T
        for j in range(3):
            row = pos_v[j:j+1, pl.ds(pl.multiple_of(s*FSUB+kk*2*CH, 2*CH), 2*CH)]
            pb_ref[kk, j] = jnp.broadcast_to(row, (128, 2*CH)).T
    def coeffs(k, n):
        cols = [[[], []] for _ in range(7)]
        for h in range(2):
            ob = [jnp.broadcast_to(obs_v[2*n+h, j:j+1, :], (16, 128)) for j in range(3)]
            for r in range(0, CH, 16):
                r0 = (k % 2)*CH + r
                d = [ob[j] - pb_ref[k//2, j, r0:r0+16, :] for j in range(3)]
                r2 = d[0]*d[0] + d[1]*d[1] + d[2]*d[2]
                inv = lax.rsqrt(r2)
                i2 = inv*inv
                i3 = (i2*inv).astype(jnp.bfloat16)
                i2 = i2.astype(jnp.bfloat16)
                db = [x.astype(jnp.bfloat16) for x in d]
                for j in range(3):
                    cols[j][h].append(db[j]*i3)
                    cols[4+j][h].append(db[j]*i2)
                cols[3][h].append(inv.astype(jnp.bfloat16))
        def whole(cs, pad):
            halves = []
            for h in range(2):
                rows = [v for c in cs for v in cols[c][h]]
                if pad: rows.append(jnp.zeros((pad, 128), jnp.bfloat16))
                halves.append(jnp.concatenate(rows, 0))
            return jnp.concatenate(halves, 1)
        return whole(range(4), 0), whole(range(4, 7), CH)
    def finish(s, u, n, p13, p2):
        for h in range(2):
            m = n*2+h
            off = off_s[me ^ m, s]
            sl = slice(h*128, h*128+128)
            p2_ref[u, m, PADR:PADR+T, :] = p2[:, sl]
            v = p13[:, sl] + p2_ref[u, m, PADR+1:PADR+T+1, :] - p2_ref[u, m, PADR-1:PADR+T-1, :]
            acc_ref[m, pl.ds(off, T), :] += v
    def cut(s):
        left = live - s*FSUB
        @pl.when(left < FSUB)
        def _():
            face = lax.broadcasted_iota(jnp.int32, (FSUB, T), 0)
            for c in range(4):
                v = src_v[s, c].astype(jnp.float32)
                src_v[s, c] = jnp.where(face < left, v, 0.0).astype(jnp.bfloat16)
    small[2].wait()
    load(0).wait()
    prep(0, 0)
    small[1].wait()
    for c in views: c.wait()
    ngrp = lax.div(nlive + U - 1, U)
    def body(i, _):
        for u in range(U):
            s = U*i + u
            nxt = jnp.minimum(s + 1, nsub - 1)
            @pl.when((s + 1 < nlive))
            def _(): load(s+1).wait()
            @pl.when((s + AHEAD < nlive))
            def _(): load(s+AHEAD).start()
            @pl.when(s + 1 < nsub)
            def _(): cut(s + 1)
        for u in range(U):
            s = U*i + u
            nxt = jnp.minimum(s + 1, nsub - 1)
            p = [[None, None] for _ in range(NT)]
            for kk in range(NP):
                if kk + 1 < NP: prep(s, kk + 1)
                else: prep(nxt, 0)
                for k in (2*kk, 2*kk+1):
                    lt = lt_ref[k]
                    for n in range(NT):
                        cs = coeffs(k, n)
                        for e in range(2):
                            y = jnp.dot(lt, cs[e], preferred_element_type=jnp.float32)
                            p[n][e] = y if k == 0 else p[n][e] + y
            for n in range(NT): finish(s, u, n, *p[n])
        return 0
    lax.fori_loop(0, ngrp, body, 0)
    for m in range(nob):
        for w in range(pw):
            out_ref[pl.ds(me ^ m, T // pw, stride=nob), w, :] = acc_ref[m, pl.ds(w, T // pw, stride=pw), :] * (1.0 / (4.0 * jnp.pi))
def face_signals(src, pos, live, off, obs, pw):
    F = src.shape[1]; T = src.shape[2]
    nob = len(obs); nsub = F // FSUB
    A = pl.BlockSpec(memory_space=pl.ANY)
    H = pl.BlockSpec(memory_space=pltpu.HBM)
    V = pl.BlockSpec(memory_space=pltpu.VMEM)
    return pl.pallas_call(
        functools.partial(signal_kernel, nob=nob, T=T, nsub=nsub, pw=pw),
        out_shape=jax.ShapeDtypeStruct((T // pw * nob, pw, 128), jnp.float32),
        in_specs=[H, H] + [A]*nob + [H, H],
        out_specs=V,
        scratch_shapes=[pltpu.SMEM(live.shape, jnp.int32), pltpu.SMEM(off.shape, jnp.int32),
                        pltpu.VMEM((nob,) + obs[0].shape, jnp.float32),
                        pltpu.VMEM(pos.shape, jnp.float32),
                        pltpu.VMEM((nsub, 4, FSUB, T), jnp.bfloat16),
                        pltpu.VMEM((FSUB//CH, T, 4*CH), jnp.bfloat16),
                        pltpu.VMEM((FSUB//CH//2, 3, 2*CH, 128), jnp.float32),
                        pltpu.VMEM((nob, T + 64, 128), jnp.float32),
                        pltpu.VMEM((U, nob, T + 2*PADR, 128), jnp.float32),
                        pltpu.SemaphoreType.DMA((3 + nob,)), pltpu.SemaphoreType.DMA((nsub,))],
        compiler_params=pltpu.CompilerParams(vmem_limit_bytes=24*1024*1024),
    )(live, off, *obs, pos, src)


def body(sources, positions, counts, offsets, observers):
    nblk = lax.axis_size("blk")
    others = [lax.ppermute(observers, "blk", [(i, i ^ m) for i in range(nblk)]) for m in range(1, nblk)]
    pieces = face_signals(sources, positions, counts, offsets.T, [observers] + others, sources.shape[2] // lax.axis_size("group"))
    arrived = lax.all_to_all(pieces, ("group", "blk"), 0, 0, tiled=True)
    return arrived.sum(0).T


def solution(mesh):
    return jax.shard_map(
        body,
        mesh=mesh,
        in_specs=(
            P(None, ("group", "blk"), None),
            P(None, ("group", "blk")),
            P(("group", "blk")),
            P(("group", "blk"), None),
            P(None, "blk"),
        ),
        out_specs=P("blk", "group"),
        check_vma=False,
    )
```

```python
import functools
import jax, jax.numpy as jnp
from jax import lax
from jax.experimental import pallas as pl
from jax.experimental.pallas import tpu as pltpu
from jax.sharding import PartitionSpec as P
FSUB=512
PADR=8
CH=64
U=2
AHEAD=4
def signal_kernel(live_hbm, off_hbm, *rest, nob, T, nsub, pw):
    obs_any = rest[:nob]
    pos_hbm, src_hbm, out_ref = rest[nob:nob+3]
    live_s, off_s, obs_v, pos_v, src_v, lt_ref, pb_ref, acc_ref, p2_ref, sem, ssem = rest[nob+3:]
    NT = nob // 2
    me = lax.axis_index("blk")
    NP = FSUB // (2*CH)
    small = [pltpu.make_async_copy(live_hbm, live_s, sem.at[0]),
             pltpu.make_async_copy(off_hbm, off_s, sem.at[1]),
             pltpu.make_async_copy(pos_hbm, pos_v, sem.at[2])]
    views = [pltpu.make_async_copy(obs_any[m], obs_v.at[m], sem.at[3+m]) for m in range(nob)]
    def load(s):
        return pltpu.make_async_copy(src_hbm.at[:, pl.ds(pl.multiple_of(s*FSUB, FSUB), FSUB), :], src_v.at[s], ssem.at[s])
    small[0].start()
    small[2].start()
    load(0).start()
    small[1].start()
    for c in views: c.start()
    load(1).start()
    acc_ref[...] = jnp.zeros_like(acc_ref)
    for m in range(nob):
        for u in range(U):
            p2_ref[u, m, 0:PADR, :] = jnp.zeros((PADR, 128), jnp.float32)
            p2_ref[u, m, PADR+T:, :] = jnp.zeros((PADR, 128), jnp.float32)
    small[0].wait()
    live = live_s[0]
    nlive = lax.div(live + FSUB - 1, FSUB)
    for s in range(2, AHEAD):
        @pl.when(s < nlive)
        def _(): load(s).start()
    def prep(s, kk):
        for e in range(2):
            f0 = (2*kk+e)*CH
            x = jnp.concatenate([src_v[s, c, f0:f0+CH, :] for c in (1, 2, 3, 0)], 0)
            lt_ref[2*kk+e] = x.T
        for j in range(3):
            row = pos_v[j:j+1, pl.ds(pl.multiple_of(s*FSUB+kk*2*CH, 2*CH), 2*CH)]
            pb_ref[kk, j] = jnp.broadcast_to(row, (128, 2*CH)).T
    def coeffs(k, n):
        cols = [[[], []] for _ in range(7)]
        for h in range(2):
            ob = [jnp.broadcast_to(obs_v[2*n+h, j:j+1, :], (16, 128)) for j in range(3)]
            for r in range(0, CH, 16):
                r0 = (k % 2)*CH + r
                d = [ob[j] - pb_ref[k//2, j, r0:r0+16, :] for j in range(3)]
                r2 = d[0]*d[0] + d[1]*d[1] + d[2]*d[2]
                inv = lax.rsqrt(r2)
                i2 = pl.reciprocal(r2, approx=True).astype(jnp.bfloat16)
                ib = inv.astype(jnp.bfloat16)
                db = [x.astype(jnp.bfloat16) for x in d]
                for j in range(3):
                    t2 = db[j]*i2
                    cols[j][h].append(t2*ib)
                    cols[4+j][h].append(t2)
                cols[3][h].append(ib)
        def whole(cs, pad):
            halves = []
            for h in range(2):
                rows = [v for c in cs for v in cols[c][h]]
                if pad: rows.append(jnp.zeros((pad, 128), jnp.bfloat16))
                halves.append(jnp.concatenate(rows, 0))
            return jnp.concatenate(halves, 1)
        return whole(range(4), 0), whole(range(4, 7), CH)
    def finish(s, u, n, p13, p2):
        for h in range(2):
            m = n*2+h
            off = off_s[me ^ m, s]
            sl = slice(h*128, h*128+128)
            p2_ref[u, m, PADR:PADR+T, :] = p2[:, sl]
            v = p13[:, sl] + p2_ref[u, m, PADR+1:PADR+T+1, :] - p2_ref[u, m, PADR-1:PADR+T-1, :]
            acc_ref[m, pl.ds(off, T), :] += v
    def cut(s):
        left = live - s*FSUB
        @pl.when(left < FSUB)
        def _():
            face = lax.broadcasted_iota(jnp.int32, (FSUB, T), 0)
            for c in range(4):
                v = src_v[s, c].astype(jnp.float32)
                src_v[s, c] = jnp.where(face < left, v, 0.0).astype(jnp.bfloat16)
    small[2].wait()
    load(0).wait()
    prep(0, 0)
    small[1].wait()
    for c in views: c.wait()
    ngrp = lax.div(nlive + U - 1, U)
    def body(i, _):
        for u in range(U):
            s = U*i + u
            nxt = jnp.minimum(s + 1, nsub - 1)
            @pl.when((s + 1 < nlive))
            def _(): load(s+1).wait()
            @pl.when((s + AHEAD < nlive))
            def _(): load(s+AHEAD).start()
            @pl.when(s + 1 < nsub)
            def _(): cut(s + 1)
        for u in range(U):
            s = U*i + u
            nxt = jnp.minimum(s + 1, nsub - 1)
            p = [[None, None] for _ in range(NT)]
            for kk in range(NP):
                if kk + 1 < NP: prep(s, kk + 1)
                else: prep(nxt, 0)
                for k in (2*kk, 2*kk+1):
                    lt = lt_ref[k]
                    for n in range(NT):
                        cs = coeffs(k, n)
                        for e in (1, 0):
                            y = jnp.dot(lt, cs[e], preferred_element_type=jnp.float32)
                            p[n][e] = y if k == 0 else p[n][e] + y
            for n in range(NT): finish(s, u, n, *p[n])
        return 0
    lax.fori_loop(0, ngrp, body, 0)
    for m in range(nob):
        for w in range(pw):
            out_ref[pl.ds(me ^ m, T // pw, stride=nob), w, :] = acc_ref[m, pl.ds(w, T // pw, stride=pw), :] * (1.0 / (4.0 * jnp.pi))
def face_signals(src, pos, live, off, obs, pw):
    F = src.shape[1]; T = src.shape[2]
    nob = len(obs); nsub = F // FSUB
    A = pl.BlockSpec(memory_space=pl.ANY)
    H = pl.BlockSpec(memory_space=pltpu.HBM)
    V = pl.BlockSpec(memory_space=pltpu.VMEM)
    return pl.pallas_call(
        functools.partial(signal_kernel, nob=nob, T=T, nsub=nsub, pw=pw),
        out_shape=jax.ShapeDtypeStruct((T // pw * nob, pw, 128), jnp.float32),
        in_specs=[H, H] + [A]*nob + [H, H],
        out_specs=V,
        scratch_shapes=[pltpu.SMEM(live.shape, jnp.int32), pltpu.SMEM(off.shape, jnp.int32),
                        pltpu.VMEM((nob,) + obs[0].shape, jnp.float32),
                        pltpu.VMEM(pos.shape, jnp.float32),
                        pltpu.VMEM((nsub, 4, FSUB, T), jnp.bfloat16),
                        pltpu.VMEM((FSUB//CH, T, 4*CH), jnp.bfloat16),
                        pltpu.VMEM((FSUB//CH//2, 3, 2*CH, 128), jnp.float32),
                        pltpu.VMEM((nob, T + 64, 128), jnp.float32),
                        pltpu.VMEM((U, nob, T + 2*PADR, 128), jnp.float32),
                        pltpu.SemaphoreType.DMA((3 + nob,)), pltpu.SemaphoreType.DMA((nsub,))],
        compiler_params=pltpu.CompilerParams(vmem_limit_bytes=54*1024*1024),
    )(live, off, *obs, pos, src)


def body(sources, positions, counts, offsets, observers):
    nblk = lax.axis_size("blk")
    others = [lax.ppermute(observers, "blk", [(i, i ^ m) for i in range(nblk)]) for m in range(1, nblk)]
    pieces = face_signals(sources, positions, counts, offsets.T, [observers] + others, sources.shape[2] // lax.axis_size("group"))
    arrived = lax.all_to_all(pieces, ("group", "blk"), 0, 0, tiled=True)
    return arrived.sum(0).T


def solution(mesh):
    return jax.shard_map(
        body,
        mesh=mesh,
        in_specs=(
            P(None, ("group", "blk"), None),
            P(None, ("group", "blk")),
            P(("group", "blk")),
            P(("group", "blk"), None),
            P(None, "blk"),
        ),
        out_specs=P("blk", "group"),
        check_vma=False,
    )
```

```python
import functools
import jax, jax.numpy as jnp
from jax import lax
from jax.experimental import pallas as pl
from jax.experimental.pallas import tpu as pltpu
from jax.sharding import PartitionSpec as P
FSUB=512
PADR=8
CH=64
U=2
AHEAD=4
def signal_kernel(live_hbm, off_hbm, *rest, nob, T, nsub, pw):
    obs_any = rest[:nob]
    pos_hbm, src_hbm, out_ref = rest[nob:nob+3]
    live_s, off_s, obs_v, pos_v, src_v, lt_ref, pb_ref, acc_ref, p2_ref, st_ref, sem, ssem = rest[nob+3:]
    NT = nob // 2
    me = lax.axis_index("blk")
    NP = FSUB // (2*CH)
    small = [pltpu.make_async_copy(live_hbm, live_s, sem.at[0]),
             pltpu.make_async_copy(off_hbm, off_s, sem.at[1]),
             pltpu.make_async_copy(pos_hbm, pos_v, sem.at[2])]
    views = [pltpu.make_async_copy(obs_any[m], obs_v.at[m], sem.at[3+m]) for m in range(nob)]
    def load(s):
        return pltpu.make_async_copy(src_hbm.at[:, pl.ds(pl.multiple_of(s*FSUB, FSUB), FSUB), :], src_v.at[s], ssem.at[s])
    small[0].start()
    small[2].start()
    load(0).start()
    small[1].start()
    for c in views: c.start()
    load(1).start()
    acc_ref[...] = jnp.zeros_like(acc_ref)
    for m in range(nob):
        for u in range(U):
            p2_ref[u, m, 0:PADR, :] = jnp.zeros((PADR, 128), jnp.float32)
            p2_ref[u, m, PADR+T:, :] = jnp.zeros((PADR, 128), jnp.float32)
    small[0].wait()
    live = live_s[0]
    nlive = lax.div(live + FSUB - 1, FSUB)
    for s in range(2, AHEAD):
        @pl.when(s < nlive)
        def _(): load(s).start()
    def prep(s, kk):
        for e in range(2):
            f0 = (2*kk+e)*CH
            x = jnp.concatenate([src_v[s, c, f0:f0+CH, :] for c in (1, 2, 3, 0)], 0)
            lt_ref[2*kk+e] = x.T
        for j in range(3):
            row = pos_v[j:j+1, pl.ds(pl.multiple_of(s*FSUB+kk*2*CH, 2*CH), 2*CH)]
            pb_ref[kk, j] = jnp.broadcast_to(row, (128, 2*CH)).T
    def coeffs(k, n):
        cols = [[[], []] for _ in range(7)]
        for h in range(2):
            ob = [jnp.broadcast_to(obs_v[2*n+h, j:j+1, :], (16, 128)) for j in range(3)]
            for r in range(0, CH, 16):
                r0 = (k % 2)*CH + r
                d = [ob[j] - pb_ref[k//2, j, r0:r0+16, :] for j in range(3)]
                r2 = d[0]*d[0] + d[1]*d[1] + d[2]*d[2]
                inv = lax.rsqrt(r2)
                i2 = pl.reciprocal(r2, approx=True).astype(jnp.bfloat16)
                ib = inv.astype(jnp.bfloat16)
                db = [x.astype(jnp.bfloat16) for x in d]
                for j in range(3):
                    t2 = db[j]*i2
                    cols[j][h].append(t2*ib)
                    cols[4+j][h].append(t2)
                cols[3][h].append(ib)
        def whole(cs, pad):
            halves = []
            for h in range(2):
                rows = [v for c in cs for v in cols[c][h]]
                if pad: rows.append(jnp.zeros((pad, 128), jnp.bfloat16))
                halves.append(jnp.concatenate(rows, 0))
            return jnp.concatenate(halves, 1)
        return whole(range(4), 0), whole(range(4, 7), CH)
    def finish(s, u, n, p13, p2):
        for h in range(2):
            m = n*2+h
            off = off_s[me ^ m, s]
            sl = slice(h*128, h*128+128)
            p2_ref[u, m, PADR:PADR+T, :] = p2[:, sl]
            v = p13[:, sl] + p2_ref[u, m, PADR+1:PADR+T+1, :] - p2_ref[u, m, PADR-1:PADR+T-1, :]
            acc_ref[m, pl.ds(off, T), :] += v
    def cut(s):
        left = live - s*FSUB
        @pl.when(left < FSUB)
        def _():
            face = lax.broadcasted_iota(jnp.int32, (FSUB, T), 0)
            for c in range(4):
                v = src_v[s, c].astype(jnp.float32)
                src_v[s, c] = jnp.where(face < left, v, 0.0).astype(jnp.bfloat16)
    small[2].wait()
    load(0).wait()
    prep(0, 0)
    small[1].wait()
    for c in views: c.wait()
    ngrp = lax.div(nlive + U - 1, U)
    def body(i, _):
        for u in range(U):
            s = U*i + u
            nxt = jnp.minimum(s + 1, nsub - 1)
            @pl.when((s + 1 < nlive))
            def _(): load(s+1).wait()
            @pl.when((s + AHEAD < nlive))
            def _(): load(s+AHEAD).start()
            @pl.when(s + 1 < nsub)
            def _(): cut(s + 1)
        for u in range(U):
            s = U*i + u
            nxt = jnp.minimum(s + 1, nsub - 1)
            p = [[None, None] for _ in range(NT)]
            for kk in range(NP):
                if kk + 1 < NP: prep(s, kk + 1)
                else: prep(nxt, 0)
                for k in (2*kk, 2*kk+1):
                    lt = lt_ref[k]
                    for n in range(NT):
                        cs = coeffs(k, n)
                        for e in (1, 0):
                            y = jnp.dot(lt, cs[e], preferred_element_type=jnp.float32)
                            p[n][e] = y if k == 0 else p[n][e] + y
            for n in range(NT): finish(s, u, n, *p[n])
        return 0
    lax.fori_loop(0, ngrp, body, 0)
    for m in range(nob):
        for w in range(pw):
            st_ref[pl.ds(me ^ m, T // pw, stride=nob), w, :] = acc_ref[m, pl.ds(w, T // pw, stride=pw), :] * (1.0 / (4.0 * jnp.pi))
    out_ref[...] = st_ref[...].astype(jnp.bfloat16)
def face_signals(src, pos, live, off, obs, pw):
    F = src.shape[1]; T = src.shape[2]
    nob = len(obs); nsub = F // FSUB
    A = pl.BlockSpec(memory_space=pl.ANY)
    H = pl.BlockSpec(memory_space=pltpu.HBM)
    V = pl.BlockSpec(memory_space=pltpu.VMEM)
    return pl.pallas_call(
        functools.partial(signal_kernel, nob=nob, T=T, nsub=nsub, pw=pw),
        out_shape=jax.ShapeDtypeStruct((T // pw * nob, pw, 128), jnp.bfloat16),
        in_specs=[H, H] + [A]*nob + [H, H],
        out_specs=V,
        scratch_shapes=[pltpu.SMEM(live.shape, jnp.int32), pltpu.SMEM(off.shape, jnp.int32),
                        pltpu.VMEM((nob,) + obs[0].shape, jnp.float32),
                        pltpu.VMEM(pos.shape, jnp.float32),
                        pltpu.VMEM((nsub, 4, FSUB, T), jnp.bfloat16),
                        pltpu.VMEM((FSUB//CH, T, 4*CH), jnp.bfloat16),
                        pltpu.VMEM((FSUB//CH//2, 3, 2*CH, 128), jnp.float32),
                        pltpu.VMEM((nob, T + 64, 128), jnp.float32),
                        pltpu.VMEM((U, nob, T + 2*PADR, 128), jnp.float32),
                        pltpu.VMEM((T // pw * nob, pw, 128), jnp.float32),
                        pltpu.SemaphoreType.DMA((3 + nob,)), pltpu.SemaphoreType.DMA((nsub,))],
        compiler_params=pltpu.CompilerParams(vmem_limit_bytes=54*1024*1024),
    )(live, off, *obs, pos, src)


def body(sources, positions, counts, offsets, observers):
    nblk = lax.axis_size("blk")
    others = [lax.ppermute(observers, "blk", [(i, i ^ m) for i in range(nblk)]) for m in range(1, nblk)]
    pieces = face_signals(sources, positions, counts, offsets.T, [observers] + others, sources.shape[2] // lax.axis_size("group"))
    arrived = lax.all_to_all(pieces, ("group", "blk"), 0, 0, tiled=True)
    return arrived.astype(jnp.float32).sum(0).T


def solution(mesh):
    return jax.shard_map(
        body,
        mesh=mesh,
        in_specs=(
            P(None, ("group", "blk"), None),
            P(None, ("group", "blk")),
            P(("group", "blk")),
            P(("group", "blk"), None),
            P(None, "blk"),
        ),
        out_specs=P("blk", "group"),
        check_vma=False,
    )
```

```python
import functools
import jax, jax.numpy as jnp
from jax import lax
from jax.experimental import pallas as pl
from jax.experimental.pallas import tpu as pltpu
from jax.sharding import PartitionSpec as P
FSUB=512
PADR=8
CH=64
U=2
AHEAD=4
def signal_kernel(*rest, nob, T, nsub, pw):
    obs_any = rest[:nob-1]
    F = nsub*FSUB
    pack_any, src_hbm, out_ref = rest[nob-1:nob+2]
    off_s, obs_v, pos_v, src_v, lt_ref, pb_ref, acc_ref, p2_ref, st_ref, sem, ssem = rest[nob+2:]
    NT = nob // 2
    me = lax.axis_index("blk")
    NP = FSUB // (2*CH)
    small = [pltpu.make_async_copy(pack_any.at[:, F+128:F+256], off_s, sem.at[0]),
             pltpu.make_async_copy(pack_any.at[:, 0:F], pos_v, sem.at[1])]
    views = [pltpu.make_async_copy(pack_any.at[:, F:F+128], obs_v.at[0], sem.at[2])]
    views += [pltpu.make_async_copy(obs_any[m-1], obs_v.at[m, 0:3], sem.at[2+m]) for m in range(1, nob)]
    def load(s):
        return pltpu.make_async_copy(src_hbm.at[:, pl.ds(pl.multiple_of(s*FSUB, FSUB), FSUB), :], src_v.at[s], ssem.at[s])
    small[0].start()
    for s in range(2): load(s).start()
    small[1].start()
    for c in views: c.start()
    acc_ref[...] = jnp.zeros_like(acc_ref)
    for m in range(nob):
        for u in range(U):
            p2_ref[u, m, 0:PADR, :] = jnp.zeros((PADR, 128), jnp.float32)
            p2_ref[u, m, PADR+T:, :] = jnp.zeros((PADR, 128), jnp.float32)
    small[0].wait()
    live = off_s[0, nsub].astype(jnp.int32)
    nlive = lax.div(live + FSUB - 1, FSUB)
    for s in range(2, AHEAD):
        @pl.when(s < nlive)
        def _(): load(s).start()
    def prep(s, kk):
        for e in range(2):
            f0 = (2*kk+e)*CH
            x = jnp.concatenate([src_v[s, c, f0:f0+CH, :] for c in (1, 2, 3, 0)], 0)
            lt_ref[2*kk+e] = x.T
        for j in range(3):
            row = pos_v[j:j+1, pl.ds(pl.multiple_of(s*FSUB+kk*2*CH, 2*CH), 2*CH)]
            pb_ref[kk, j] = jnp.broadcast_to(row, (128, 2*CH)).T
    def coeffs(k, n):
        cols = [[[], []] for _ in range(7)]
        for h in range(2):
            ob = [jnp.broadcast_to(obs_v[2*n+h, j:j+1, :], (16, 128)) for j in range(3)]
            for r in range(0, CH, 16):
                r0 = (k % 2)*CH + r
                d = [ob[j] - pb_ref[k//2, j, r0:r0+16, :] for j in range(3)]
                r2 = d[0]*d[0] + d[1]*d[1] + d[2]*d[2]
                inv = lax.rsqrt(r2)
                i2 = pl.reciprocal(r2, approx=True).astype(jnp.bfloat16)
                ib = inv.astype(jnp.bfloat16)
                db = [x.astype(jnp.bfloat16) for x in d]
                for j in range(3):
                    t2 = db[j]*i2
                    cols[j][h].append(t2*ib)
                    cols[4+j][h].append(t2)
                cols[3][h].append(ib)
        def whole(cs, pad):
            halves = []
            for h in range(2):
                rows = [v for c in cs for v in cols[c][h]]
                if pad: rows.append(jnp.zeros((pad, 128), jnp.bfloat16))
                halves.append(jnp.concatenate(rows, 0))
            return jnp.concatenate(halves, 1)
        return whole(range(4), 0), whole(range(4, 7), CH)
    def finish(s, u, n, p13, p2):
        for h in range(2):
            m = n*2+h
            off = off_s[me ^ m, s].astype(jnp.int32)
            sl = slice(h*128, h*128+128)
            p2_ref[u, m, PADR:PADR+T, :] = p2[:, sl]
            v = p13[:, sl] + p2_ref[u, m, PADR+1:PADR+T+1, :] - p2_ref[u, m, PADR-1:PADR+T-1, :]
            acc_ref[m, pl.ds(off, T), :] += v
    def cut(s):
        left = live - s*FSUB
        @pl.when(left < FSUB)
        def _():
            face = lax.broadcasted_iota(jnp.int32, (FSUB, T), 0)
            for c in range(4):
                v = src_v[s, c].astype(jnp.float32)
                src_v[s, c] = jnp.where(face < left, v, 0.0).astype(jnp.bfloat16)
    small[1].wait()
    load(0).wait()
    prep(0, 0)
    for c in views: c.wait()
    ngrp = lax.div(nlive + U - 1, U)
    def body(i, _):
        for u in range(U):
            s = U*i + u
            nxt = jnp.minimum(s + 1, nsub - 1)
            @pl.when((s + 1 < nlive))
            def _(): load(s+1).wait()
            @pl.when((s + AHEAD < nlive))
            def _(): load(s+AHEAD).start()
            @pl.when(s + 1 < nsub)
            def _(): cut(s + 1)
        for u in range(U):
            s = U*i + u
            nxt = jnp.minimum(s + 1, nsub - 1)
            p = [[None, None] for _ in range(NT)]
            for kk in range(NP):
                if kk + 1 < NP: prep(s, kk + 1)
                else: prep(nxt, 0)
                for k in (2*kk, 2*kk+1):
                    lt = lt_ref[k]
                    for n in range(NT):
                        cs = coeffs(k, n)
                        for e in (1, 0):
                            y = jnp.dot(lt, cs[e], preferred_element_type=jnp.float32)
                            p[n][e] = y if k == 0 else p[n][e] + y
            for n in range(NT): finish(s, u, n, *p[n])
        return 0
    lax.fori_loop(0, ngrp, body, 0)
    for m in range(nob):
        for w in range(pw):
            st_ref[pl.ds(me ^ m, T // pw, stride=nob), w, :] = acc_ref[m, pl.ds(w, T // pw, stride=pw), :] * (1.0 / (4.0 * jnp.pi))
    out_ref[...] = st_ref[...].astype(jnp.bfloat16)
def face_signals(src, obs, pack, pw):
    F = src.shape[1]; T = src.shape[2]
    nob = len(obs) + 1; nsub = F // FSUB
    A = pl.BlockSpec(memory_space=pl.ANY)
    H = pl.BlockSpec(memory_space=pltpu.HBM)
    V = pl.BlockSpec(memory_space=pltpu.VMEM)
    return pl.pallas_call(
        functools.partial(signal_kernel, nob=nob, T=T, nsub=nsub, pw=pw),
        out_shape=jax.ShapeDtypeStruct((T // pw * nob, pw, 128), jnp.bfloat16),
        in_specs=[A]*(nob - 1) + [A, H],
        out_specs=V,
        scratch_shapes=[pltpu.SMEM((4, 128), jnp.float32),
                        pltpu.VMEM((nob, 4, 128), jnp.float32),
                        pltpu.VMEM((4, F), jnp.float32),
                        pltpu.VMEM((nsub, 4, FSUB, T), jnp.bfloat16),
                        pltpu.VMEM((FSUB//CH, T, 4*CH), jnp.bfloat16),
                        pltpu.VMEM((FSUB//CH//2, 3, 2*CH, 128), jnp.float32),
                        pltpu.VMEM((nob, T + 64, 128), jnp.float32),
                        pltpu.VMEM((U, nob, T + 2*PADR, 128), jnp.float32),
                        pltpu.VMEM((T // pw * nob, pw, 128), jnp.float32),
                        pltpu.SemaphoreType.DMA((2 + nob,)), pltpu.SemaphoreType.DMA((nsub,))],
        compiler_params=pltpu.CompilerParams(vmem_limit_bytes=50*1024*1024),
    )(*obs, pack, src)


def body(sources, positions, counts, offsets, observers):
    nblk = lax.axis_size("blk")
    others = [lax.ppermute(observers, "blk", [(i, i ^ m) for i in range(nblk)]) for m in range(1, nblk)]
    nsub = offsets.shape[0]
    spot = lax.broadcasted_iota(jnp.int32, (nblk, 128), 1)
    shifts = jnp.pad(offsets.T, ((0, 0), (0, 128 - nsub)))
    numbers = jnp.where(spot == nsub, counts[0], shifts).astype(jnp.float32)
    pack = jnp.concatenate([jnp.pad(positions, ((0, 1), (0, 0))), jnp.pad(observers, ((0, 1), (0, 0))), numbers], 1)
    pieces = face_signals(sources, others, pack, sources.shape[2] // lax.axis_size("group"))
    arrived = lax.all_to_all(pieces, ("group", "blk"), 0, 0, tiled=True)
    return arrived.astype(jnp.float32).sum(0).T


def solution(mesh):
    return jax.shard_map(
        body,
        mesh=mesh,
        in_specs=(
            P(None, ("group", "blk"), None),
            P(None, ("group", "blk")),
            P(("group", "blk")),
            P(("group", "blk"), None),
            P(None, "blk"),
        ),
        out_specs=P("blk", "group"),
        check_vma=False,
    )
```

```python
import functools
import jax, jax.numpy as jnp
from jax import lax
from jax.experimental import pallas as pl
from jax.experimental.pallas import tpu as pltpu
from jax.sharding import PartitionSpec as P
FSUB=512
PADR=8
CH=64
U=2
AHEAD=4
def signal_kernel(*rest, nob, T, nsub, pw):
    obs_any = rest[:nob-1]
    F = nsub*FSUB
    pack_any, num_any, src_hbm, out_ref = rest[nob-1:nob+3]
    off_s, obs_v, pos_v, src_v, lt_ref, pb_ref, acc_ref, p2_ref, st_ref, sem, ssem = rest[nob+3:]
    NT = nob // 2
    me = lax.axis_index("blk")
    NP = FSUB // (2*CH)
    small = [pltpu.make_async_copy(num_any, off_s, sem.at[0]),
             pltpu.make_async_copy(pack_any.at[:, 0:F], pos_v, sem.at[1])]
    views = [pltpu.make_async_copy(pack_any.at[:, F:F+128], obs_v.at[0], sem.at[2])]
    views += [pltpu.make_async_copy(obs_any[m-1], obs_v.at[m, 0:3], sem.at[2+m]) for m in range(1, nob)]
    def load(s):
        return pltpu.make_async_copy(src_hbm.at[:, pl.ds(pl.multiple_of(s*FSUB, FSUB), FSUB), :], src_v.at[s], ssem.at[s])
    first = [pltpu.make_async_copy(src_hbm.at[:, a:b, :], src_v.at[0, :, a:b, :], sem.at[c])
             for a, b, c in ((0, 2*CH, 2 + nob), (2*CH, FSUB, 3 + nob))]
    first[0].start()
    small[0].start()
    small[1].start()
    for c in views: c.start()
    first[1].start()
    load(1).start()
    acc_ref[...] = jnp.zeros_like(acc_ref)
    for m in range(nob):
        for u in range(U):
            p2_ref[u, m, 0:PADR, :] = jnp.zeros((PADR, 128), jnp.float32)
            p2_ref[u, m, PADR+T:, :] = jnp.zeros((PADR, 128), jnp.float32)
    small[0].wait()
    live = off_s[0, nsub].astype(jnp.int32)
    nlive = lax.div(live + FSUB - 1, FSUB)
    for s in range(2, AHEAD):
        @pl.when(s < nlive)
        def _(): load(s).start()
    def prep(s, kk):
        for e in range(2):
            f0 = (2*kk+e)*CH
            x = jnp.concatenate([src_v[s, c, f0:f0+CH, :] for c in (1, 2, 3, 0)], 0)
            lt_ref[2*kk+e] = x.T
        for j in range(3):
            row = pos_v[j:j+1, pl.ds(pl.multiple_of(s*FSUB+kk*2*CH, 2*CH), 2*CH)]
            pb_ref[kk, j] = jnp.broadcast_to(row, (128, 2*CH)).T
    def coeffs(k, n):
        cols = [[[], []] for _ in range(7)]
        for h in range(2):
            ob = [jnp.broadcast_to(obs_v[2*n+h, j:j+1, :], (16, 128)) for j in range(3)]
            for r in range(0, CH, 16):
                r0 = (k % 2)*CH + r
                d = [ob[j] - pb_ref[k//2, j, r0:r0+16, :] for j in range(3)]
                r2 = d[0]*d[0] + d[1]*d[1] + d[2]*d[2]
                inv = lax.rsqrt(r2)
                i2 = pl.reciprocal(r2, approx=True).astype(jnp.bfloat16)
                ib = inv.astype(jnp.bfloat16)
                db = [x.astype(jnp.bfloat16) for x in d]
                for j in range(3):
                    t2 = db[j]*i2
                    cols[j][h].append(t2*ib)
                    cols[4+j][h].append(t2)
                cols[3][h].append(ib)
        def whole(cs, pad):
            halves = []
            for h in range(2):
                rows = [v for c in cs for v in cols[c][h]]
                if pad: rows.append(jnp.zeros((pad, 128), jnp.bfloat16))
                halves.append(jnp.concatenate(rows, 0))
            return jnp.concatenate(halves, 1)
        return whole(range(4), 0), whole(range(4, 7), CH)
    def finish(s, u, n, p13, p2):
        for h in range(2):
            m = n*2+h
            off = off_s[me ^ m, s].astype(jnp.int32)
            sl = slice(h*128, h*128+128)
            p2_ref[u, m, PADR:PADR+T, :] = p2[:, sl]
            v = p13[:, sl] + p2_ref[u, m, PADR+1:PADR+T+1, :] - p2_ref[u, m, PADR-1:PADR+T-1, :]
            acc_ref[m, pl.ds(off, T), :] += v
    def cut(s):
        left = live - s*FSUB
        @pl.when(left < FSUB)
        def _():
            face = lax.broadcasted_iota(jnp.int32, (FSUB, T), 0)
            for c in range(4):
                v = src_v[s, c].astype(jnp.float32)
                src_v[s, c] = jnp.where(face < left, v, 0.0).astype(jnp.bfloat16)
    small[1].wait()
    first[0].wait()
    prep(0, 0)
    first[1].wait()
    for c in views: c.wait()
    ngrp = lax.div(nlive + U - 1, U)
    def body(i, _):
        for u in range(U):
            s = U*i + u
            nxt = jnp.minimum(s + 1, nsub - 1)
            @pl.when((s + 1 < nlive))
            def _(): load(s+1).wait()
            @pl.when((s + AHEAD < nlive))
            def _(): load(s+AHEAD).start()
            @pl.when(s + 1 < nsub)
            def _(): cut(s + 1)
        for u in range(U):
            s = U*i + u
            nxt = jnp.minimum(s + 1, nsub - 1)
            p = [[None, None] for _ in range(NT)]
            for kk in range(NP):
                if kk + 1 < NP: prep(s, kk + 1)
                else: prep(nxt, 0)
                for k in (2*kk, 2*kk+1):
                    lt = lt_ref[k]
                    for n in range(NT):
                        cs = coeffs(k, n)
                        for e in (1, 0):
                            y = jnp.dot(lt, cs[e], preferred_element_type=jnp.float32)
                            p[n][e] = y if k == 0 else p[n][e] + y
            for n in range(NT): finish(s, u, n, *p[n])
        return 0
    lax.fori_loop(0, ngrp, body, 0)
    for m in range(nob):
        for w in range(pw):
            st_ref[pl.ds(me ^ m, T // pw, stride=nob), w, :] = acc_ref[m, pl.ds(w, T // pw, stride=pw), :] * (1.0 / (4.0 * jnp.pi))
    out_ref[...] = st_ref[...].astype(jnp.bfloat16)
def face_signals(src, obs, pack, numbers, pw):
    F = src.shape[1]; T = src.shape[2]
    nob = len(obs) + 1; nsub = F // FSUB
    A = pl.BlockSpec(memory_space=pl.ANY)
    H = pl.BlockSpec(memory_space=pltpu.HBM)
    V = pl.BlockSpec(memory_space=pltpu.VMEM)
    return pl.pallas_call(
        functools.partial(signal_kernel, nob=nob, T=T, nsub=nsub, pw=pw),
        out_shape=jax.ShapeDtypeStruct((T // pw * nob, pw, 128), jnp.bfloat16),
        in_specs=[A]*(nob - 1) + [A, A, H],
        out_specs=V,
        scratch_shapes=[pltpu.SMEM((4, 128), jnp.float32),
                        pltpu.VMEM((nob, 4, 128), jnp.float32),
                        pltpu.VMEM((4, F), jnp.float32),
                        pltpu.VMEM((nsub, 4, FSUB, T), jnp.bfloat16),
                        pltpu.VMEM((FSUB//CH, T, 4*CH), jnp.bfloat16),
                        pltpu.VMEM((FSUB//CH//2, 3, 2*CH, 128), jnp.float32),
                        pltpu.VMEM((nob, T + 64, 128), jnp.float32),
                        pltpu.VMEM((U, nob, T + 2*PADR, 128), jnp.float32),
                        pltpu.VMEM((T // pw * nob, pw, 128), jnp.float32),
                        pltpu.SemaphoreType.DMA((4 + nob,)), pltpu.SemaphoreType.DMA((nsub,))],
        compiler_params=pltpu.CompilerParams(vmem_limit_bytes=50*1024*1024),
    )(*obs, pack, numbers, src)


def body(sources, positions, counts, offsets, observers):
    nblk = lax.axis_size("blk")
    others = [lax.ppermute(observers, "blk", [(i, i ^ m) for i in range(nblk)]) for m in range(1, nblk)]
    nsub = offsets.shape[0]
    shifts = jnp.pad(offsets.T, ((0, 0), (0, 128 - nsub)))
    live = jnp.pad(counts.reshape(1, 1), ((0, nblk - 1), (nsub, 127 - nsub)))
    numbers = (shifts + live).astype(jnp.float32)
    pack = jnp.concatenate([jnp.pad(positions, ((0, 1), (0, 0))), jnp.pad(observers, ((0, 1), (0, 0)))], 1)
    pieces = face_signals(sources, others, pack, numbers, sources.shape[2] // lax.axis_size("group"))
    arrived = lax.all_to_all(pieces, ("group", "blk"), 0, 0, tiled=True)
    return arrived.astype(jnp.float32).sum(0).T


def solution(mesh):
    return jax.shard_map(
        body,
        mesh=mesh,
        in_specs=(
            P(None, ("group", "blk"), None),
            P(None, ("group", "blk")),
            P(("group", "blk")),
            P(("group", "blk"), None),
            P(None, "blk"),
        ),
        out_specs=P("blk", "group"),
        check_vma=False,
    )
```
